512 devices in a mesh: blk: 32 (over x, z_lo, core), grp: 16 (over y, z_hi).
Axes of the slice: x: 4, y: 4, z: 16 (z_hi: 4, z_lo: 4; z = z_hi * 4 + z_lo), core: 2. Of those that a mesh axis runs over, the one named last changes fastest.
Arguments:
- points: float32 [9, 65536], P(None, ('blk', 'grp')), may hold values from -6 to 6
- inv_length: float32 [9], replicated, may hold values from 0.6 to 1.2
- probes: float32 [32, 65536], P(None, ('blk', 'grp')), may hold values from -6 to 6
- noise: float32 [1], replicated, may hold values from 0.2 to 1
Outputs:
- product: float32 [32, 65536], P(None, ('blk', 'grp'))
The draws below stay inside these ranges and needn't reach their ends.
All inputs are finite; a program needn't handle non-finite values.
Results may differ from the reference program's by a relative error of at most 0.0003.
Values sent between devices are 32-bit elements; how exact they have to be, the bound alone decides.
No kernel may reach another device: no remote copies, remote signals or barrier semaphores. Data moves between devices by JAX's collectives and lax.ppermute only.
A program may use at most 64 MiB of HBM per device.

```python
import math
import jax
import jax.numpy as jnp
from jax import lax

DIMS = 9
NPROBE = 32
NPTS = 65536


def steps_of(stream_key, extent, cuts, smallest, high):
    factor_of, own = 1.0, jax.random.fold_in(stream_key, 6)
    for axis_at, blocks in cuts:
        steps = jnp.exp(jax.random.uniform(jax.random.fold_in(own, axis_at), (blocks,), jnp.float32, smallest / len(cuts), high / len(cuts)))
        factor_of = factor_of * jnp.repeat(steps, extent[axis_at] // blocks).reshape([-1 if axis == axis_at else 1 for axis in range(len(extent))])
    return factor_of


def bell_draw(stream_key, shape, scale, most, shards=(), held_as=jnp.bfloat16):
    entries = scale * jax.random.normal(stream_key, shape, jnp.float32)
    if shards:
        entries = entries * steps_of(stream_key, shape, shards, -0.22, 0.18)
    return jnp.clip(entries, -most, most).astype(held_as)


def setup_inputs(seed: int = 0) -> dict:
    key_of = jax.random.split(jax.random.key(seed), 5)
    return {
        "points": bell_draw(key_of[0], (DIMS, NPTS), 1.0, 6.0, ((1, 512),), jnp.float32),
        "inv_length": jnp.clip(jnp.exp(jax.random.uniform(key_of[1], (DIMS,), jnp.float32, math.log(0.6), math.log(1.2))), 0.6, 1.2),
        "probes": bell_draw(key_of[2], (NPROBE, NPTS), 1.0, 6.0, ((1, 512),), jnp.float32),
        "noise": jnp.clip(jnp.exp(jax.random.uniform(key_of[3], (1,), jnp.float32, math.log(0.2), math.log(1.0))), 0.2, 1.0),
    }


ROOT_FIVE = math.sqrt(5.0)

def matern_tile(rows, cols):
    squared = jnp.zeros((rows.shape[1], cols.shape[1]), jnp.float32)
    for coord in range(rows.shape[0]):
        spread = rows[coord][:, None] - cols[coord][None, :]
        squared = squared + spread * spread
    scaled_r = ROOT_FIVE * jnp.sqrt(squared)
    return (1.0 + scaled_r + scaled_r * scaled_r / 3.0) * jnp.exp(-scaled_r)

def reference(points, inv_length, probes, noise):
    scaled = points * inv_length[:, None]
    total = scaled.shape[1]
    rows = math.gcd(total, 512)
    blocks = scaled.reshape(scaled.shape[0], total // rows, rows).transpose(1, 0, 2)
    probes_t = probes.T

    def one_block(block):
        tile = matern_tile(block, scaled)
        return jnp.dot(tile, probes_t, preferred_element_type=jnp.float32, precision=lax.Precision.HIGHEST)
    parts = lax.map(one_block, blocks)
    product = parts.reshape(total, probes.shape[0]).T
    return product + noise[0] * probes
```

```python
import functools
import math

import jax
import jax.numpy as jnp
from jax import lax
from jax.experimental import pallas as pl
from jax.experimental.pallas import tpu as pltpu
from jax.sharding import Mesh, PartitionSpec as P

AXES = ("x", "zl", "c", "y", "zh")
COL_AXES = ("zl", "zh")
ROW_AXES = ("x", "y")
LANES = 128
UNIT = 16
DEPTH = 128
TILE = 256
STEP = 32
SCALE = math.sqrt(5.0) / 3.0
RATE = -3.0 / math.log(2.0)
TINY = 1e-30
PREPARE_LIMIT = 60 * 1024 * 1024
LIMIT = 32 * 1024 * 1024
WHOLE = pl.BlockSpec(memory_space=pltpu.VMEM)


def extended(x, norm, one, ref):
    dims = x.shape[0]
    ref[...] = jnp.zeros(ref.shape, jnp.float32)
    ref[0:dims] = x
    ref[dims : dims + 1] = norm
    ref[dims + 1 : dims + 2] = one


def prepare_kernel(points_ref, length_ref, probes_ref, row_ref, cols_ref):
    dims, n_probes = points_ref.shape[0], probes_ref.shape[0]
    at = lax.broadcasted_iota(jnp.int32, (dims, dims), 0) == lax.broadcasted_iota(jnp.int32, (dims, dims), 1)
    length = jnp.sum(jnp.where(at, length_ref[...], 0.0), axis=1, keepdims=True)
    x = points_ref[...] * (length * SCALE)
    norm = jnp.sum(x * x, axis=0, keepdims=True)
    extended(x, norm, jnp.ones_like(norm), row_ref)
    probes = probes_ref[...]
    for start in range(0, cols_ref.shape[0], dims + n_probes):
        cols_ref[start : start + dims] = x
        cols_ref[start + dims : start + dims + n_probes] = probes


def split3(value):
    first = value.astype(jnp.bfloat16)
    rest = value - first.astype(jnp.float32)
    second = rest.astype(jnp.bfloat16)
    third = (rest - second.astype(jnp.float32)).astype(jnp.bfloat16)
    return first, second, third


def halves(squared):
    squared = jnp.maximum(squared, TINY)
    v = squared * lax.rsqrt(squared)
    k = ((squared + v) + (1.0 / 3.0)) * jnp.exp2(v * RATE)
    high = k.astype(jnp.bfloat16)
    return high, (k - high.astype(jnp.float32)).astype(jnp.bfloat16)


def block_kernel(last, dims, *refs):
    if last:
        a, cols_ref, sum_ref, out_ref, b, q, unit, d0, d1, h0, h1, acc = refs
        n_probes = out_ref.shape[1]
    else:
        rows_ref, cols_ref, acc, a, b, q, unit, d0, d1, h0, h1 = refs
        n_probes = acc.shape[1] // 2
    d, h = (d0, d1), (h0, h1)
    per = dims + n_probes
    n_rows, n_cols = a.shape[0] * TILE // LANES, cols_ref.shape[0] // per
    each = TILE // LANES
    zero = jnp.zeros((UNIT, LANES), jnp.bfloat16)

    if not last:
        for s in range(n_rows):
            u1, u2, u3 = split3(rows_ref[s])
            lanes = slice((s % each) * LANES, (s % each + 1) * LANES)
            a[s // each, :, lanes] = jnp.concatenate([u1, u1, u2, u2, u1, u3, zero, zero], axis=0)
    for s in range(n_cols):
        x = cols_ref[s * per : s * per + dims]
        norm = jnp.sum(x * x, axis=0, keepdims=True)
        extended(-2.0 * x, jnp.ones_like(norm), norm, unit.at[s])
        v1, v2, v3 = split3(unit[s])
        lanes = slice((s % each) * LANES, (s % each + 1) * LANES)
        stack = jnp.concatenate([v1, v2, v1, v2, v3, v1, zero, zero], axis=0)
        b[s // each, lanes, :] = stack.T
        p = cols_ref[s * per + dims : (s + 1) * per]
        p1 = p.astype(jnp.bfloat16)
        p2 = (p - p1.astype(jnp.float32)).astype(jnp.bfloat16)
        both = jnp.concatenate([p1, p2], axis=0)
        q[s // each, :, lanes] = both
        q[s // each, :, lanes.start + TILE : lanes.stop + TILE] = both
    acc[...] = sum_ref[...] if last else jnp.zeros_like(acc)
    tiles, chunks = a.shape[0], b.shape[0]

    chain = 4 if last else 2

    def strip(i, carry):
        for at in range(chain * tiles):
            chunk, tile = i * chain + at // tiles, at % tiles
            now, then = at % 2, 1 - at % 2
            before = chunk if tile > 0 else jnp.maximum(chunk - 1, 0)
            after = chunk if tile + 1 < tiles else jnp.minimum(chunk + 1, chunks - 1)
            product = jnp.dot(q[before], h[then][...], preferred_element_type=jnp.float32)
            ahead = jnp.dot(b[after], a[(tile + 1) % tiles], preferred_element_type=jnp.float32)
            acc[(tile - 1) % tiles] += product
            d[then][...] = ahead
            for start in range(0, TILE, STEP):
                high, low = halves(d[now][start : start + STEP])
                h[now][start : start + STEP] = high
                h[now][TILE + start : TILE + start + STEP] = low
        return carry

    h1[...] = jnp.zeros_like(h1)
    d0[...] = jnp.dot(b[0], a[0], preferred_element_type=jnp.float32)
    lax.fori_loop(0, chunks // chain, strip, 0)
    acc[tiles - 1] += jnp.dot(q[chunks - 1], h[(tiles - 1) % 2][...], preferred_element_type=jnp.float32)
    if not last:
        return
    for s in range(n_rows):
        lanes = slice((s % each) * LANES, (s % each + 1) * LANES)
        out_ref[s] = 3.0 * (acc[s // each, 0:n_probes, lanes] + acc[s // each, n_probes:, lanes])


def block(rows, cols, dims, n_probes, total=None):
    f32, bf16 = jnp.float32, jnp.bfloat16
    last = total is not None
    n_rows = rows.shape[0] * TILE // LANES if last else rows.shape[0]
    n_cols = cols.shape[0] // (dims + n_probes)
    row_tiles, col_tiles = n_rows * LANES // TILE, n_cols * LANES // TILE
    sums = jax.ShapeDtypeStruct((row_tiles, 2 * n_probes, TILE), f32)
    turned = jax.ShapeDtypeStruct((row_tiles, DEPTH, TILE), bf16)
    entries = n_rows * n_cols * LANES * LANES
    return pl.pallas_call(
        functools.partial(block_kernel, last, dims),
        out_shape=jax.ShapeDtypeStruct((n_rows, n_probes, LANES), f32) if last else (sums, turned),
        in_specs=[WHOLE] * (3 if last else 2),
        out_specs=WHOLE if last else (WHOLE, WHOLE),
        scratch_shapes=[
            pltpu.VMEM((col_tiles, TILE, DEPTH), bf16),
            pltpu.VMEM((col_tiles, 2 * n_probes, 2 * TILE), bf16),
            pltpu.VMEM((n_cols, UNIT, LANES), f32),
            pltpu.VMEM((TILE, TILE), f32),
            pltpu.VMEM((TILE, TILE), f32),
            pltpu.VMEM((2 * TILE, TILE), bf16),
            pltpu.VMEM((2 * TILE, TILE), bf16),
        ]
        + [pltpu.VMEM(sums.shape, f32)] * last,
        compiler_params=pltpu.CompilerParams(vmem_limit_bytes=LIMIT),
        cost_estimate=pl.CostEstimate(flops=entries * 2000, bytes_accessed=4 * cols.size, transcendentals=2 * entries),
        name="block_last" if last else "block_first",
    )(*((rows, cols, total) if last else (rows, cols)))


def body(points, inv_length, probes, noise):
    n_cols = lax.axis_size(COL_AXES)
    (dims, width), n_probes = points.shape, probes.shape[0]
    per = dims + n_probes
    f32 = jnp.float32
    row, cols = pl.pallas_call(
        prepare_kernel,
        out_shape=(
            jax.ShapeDtypeStruct((UNIT, width), f32),
            jax.ShapeDtypeStruct((n_cols * per, width), f32),
        ),
        in_specs=[WHOLE] * 3,
        out_specs=(WHOLE, WHOLE),
        compiler_params=pltpu.CompilerParams(vmem_limit_bytes=PREPARE_LIMIT),
        name="prepare",
    )(points, inv_length[None, :], probes)
    cols = lax.all_to_all(cols.reshape(n_cols * per, 1, width), COL_AXES, 0, 0, tiled=True).reshape(n_cols * per, width)
    other = lax.ppermute(cols, "c", [(0, 1), (1, 0)])
    rows = lax.all_gather(row, ROW_AXES, axis=0)
    total, turned = block(rows, cols, dims, n_probes)
    part = block(turned, other, dims, n_probes, total)
    part = lax.all_to_all(part, ROW_AXES, 0, 0, tiled=True)
    return jnp.sum(part, axis=0) + noise[0] * probes


def solution(mesh):
    fine = Mesh(mesh.devices.reshape(4, 4, 2, 4, 4), AXES)
    split = P(None, AXES)
    return jax.shard_map(body, mesh=fine, in_specs=(split, P(), split, P()), out_specs=split, check_vma=False)
```

```python
import functools
import math

import jax
import jax.numpy as jnp
from jax import lax
from jax.experimental import pallas as pl
from jax.experimental.pallas import tpu as pltpu
from jax.sharding import Mesh, PartitionSpec as P

AXES = ("x", "zl", "c", "y", "zh")
COL_AXES = ("zl", "zh")
ROW_AXES = ("x", "y")
LANES = 128
UNIT = 16
DEPTH = 128
TILE = 256
STEP = 32
SCALE = math.sqrt(5.0) / 3.0
RATE = -3.0 / math.log(2.0)
TINY = 1e-30
PREPARE_LIMIT = 60 * 1024 * 1024
LIMIT = 32 * 1024 * 1024
WHOLE = pl.BlockSpec(memory_space=pltpu.VMEM)


def extended(x, norm, one, ref):
    dims = x.shape[0]
    ref[...] = jnp.zeros(ref.shape, jnp.float32)
    ref[0:dims] = x
    ref[dims : dims + 1] = norm
    ref[dims + 1 : dims + 2] = one


def prepare_kernel(points_ref, length_ref, probes_ref, row_ref, cols_ref):
    dims, n_probes = points_ref.shape[0], probes_ref.shape[0]
    at = lax.broadcasted_iota(jnp.int32, (dims, dims), 0) == lax.broadcasted_iota(jnp.int32, (dims, dims), 1)
    length = jnp.sum(jnp.where(at, length_ref[...], 0.0), axis=1, keepdims=True)
    x = points_ref[...] * (length * SCALE)
    norm = jnp.sum(x * x, axis=0, keepdims=True)
    extended(x, norm, jnp.ones_like(norm), row_ref)
    probes = probes_ref[...]
    for start in range(0, cols_ref.shape[0], dims + n_probes):
        cols_ref[start : start + dims] = x
        cols_ref[start + dims : start + dims + n_probes] = probes


def split3(value):
    first = value.astype(jnp.bfloat16)
    rest = value - first.astype(jnp.float32)
    second = rest.astype(jnp.bfloat16)
    third = (rest - second.astype(jnp.float32)).astype(jnp.bfloat16)
    return first, second, third


def halves(squared):
    squared = jnp.maximum(squared, TINY)
    v = squared * lax.rsqrt(squared)
    k = ((squared + v) + (1.0 / 3.0)) * jnp.exp2(v * RATE)
    high = k.astype(jnp.bfloat16)
    return high, (k - high.astype(jnp.float32)).astype(jnp.bfloat16)


def block_kernel(last, dims, *refs):
    if last:
        a, cols_ref, sum_ref, out_ref, b, q, unit, d0, d1, h0, h1, acc = refs
        n_probes = out_ref.shape[1]
    else:
        rows_ref, cols_ref, acc, a, b, q, unit, d0, d1, h0, h1 = refs
        n_probes = acc.shape[1] // 2
    d, h = (d0, d1), (h0, h1)
    per = dims + n_probes
    n_rows, n_cols = a.shape[0] * TILE // LANES, cols_ref.shape[0] // per
    each = TILE // LANES
    zero = jnp.zeros((UNIT, LANES), jnp.bfloat16)

    if not last:
        for s in range(n_rows):
            u1, u2, u3 = split3(rows_ref[s])
            lanes = slice((s % each) * LANES, (s % each + 1) * LANES)
            a[s // each, :, lanes] = jnp.concatenate([u1, u1, u2, u2, u1, u3, zero, zero], axis=0)
    for s in range(n_cols):
        x = cols_ref[s * per : s * per + dims]
        norm = jnp.sum(x * x, axis=0, keepdims=True)
        extended(-2.0 * x, jnp.ones_like(norm), norm, unit.at[s])
        v1, v2, v3 = split3(unit[s])
        lanes = slice((s % each) * LANES, (s % each + 1) * LANES)
        stack = jnp.concatenate([v1, v2, v1, v2, v3, v1, zero, zero], axis=0)
        b[s // each, lanes, :] = stack.T
        p = cols_ref[s * per + dims : (s + 1) * per]
        p1 = p.astype(jnp.bfloat16)
        p2 = (p - p1.astype(jnp.float32)).astype(jnp.bfloat16)
        both = jnp.concatenate([p1, p2], axis=0)
        q[s // each, :, lanes] = both
        q[s // each, :, lanes.start + TILE : lanes.stop + TILE] = both
    tiles, chunks = a.shape[0], b.shape[0]
    count = tiles * chunks

    def distance(at):
        return jnp.dot(b[at // tiles], a[at % tiles], preferred_element_type=jnp.float32)

    def product(at):
        return jnp.dot(q[at // tiles], h[at % 2][...], preferred_element_type=jnp.float32)

    def add(at, value):
        tile = at % tiles
        if at >= tiles:
            value = acc[tile] + value
        elif last:
            value = sum_ref[tile] + value
        if not last or at < count - tiles:
            acc[tile] = value
            return
        value = 3.0 * (value[0:n_probes] + value[n_probes:])
        for s in range(each):
            out_ref[tile * each + s] = value[:, s * LANES : (s + 1) * LANES]

    d0[...] = distance(0)
    for at in range(count):
        now, then = at % 2, 1 - at % 2
        if at > 0:
            add(at - 1, product(at - 1))
        if at + 1 < count:
            d[then][...] = distance(at + 1)
        for start in range(0, TILE, STEP):
            high, low = halves(d[now][start : start + STEP])
            h[now][start : start + STEP] = high
            h[now][TILE + start : TILE + start + STEP] = low
    add(count - 1, product(count - 1))


def block(rows, cols, dims, n_probes, total=None):
    f32, bf16 = jnp.float32, jnp.bfloat16
    last = total is not None
    n_rows = rows.shape[0] * TILE // LANES if last else rows.shape[0]
    n_cols = cols.shape[0] // (dims + n_probes)
    row_tiles, col_tiles = n_rows * LANES // TILE, n_cols * LANES // TILE
    sums = jax.ShapeDtypeStruct((row_tiles, 2 * n_probes, TILE), f32)
    turned = jax.ShapeDtypeStruct((row_tiles, DEPTH, TILE), bf16)
    entries = n_rows * n_cols * LANES * LANES
    return pl.pallas_call(
        functools.partial(block_kernel, last, dims),
        out_shape=jax.ShapeDtypeStruct((n_rows, n_probes, LANES), f32) if last else (sums, turned),
        in_specs=[WHOLE] * (3 if last else 2),
        out_specs=WHOLE if last else (WHOLE, WHOLE),
        scratch_shapes=[
            pltpu.VMEM((col_tiles, TILE, DEPTH), bf16),
            pltpu.VMEM((col_tiles, 2 * n_probes, 2 * TILE), bf16),
            pltpu.VMEM((n_cols, UNIT, LANES), f32),
            pltpu.VMEM((TILE, TILE), f32),
            pltpu.VMEM((TILE, TILE), f32),
            pltpu.VMEM((2 * TILE, TILE), bf16),
            pltpu.VMEM((2 * TILE, TILE), bf16),
        ]
        + [pltpu.VMEM(sums.shape, f32)] * last,
        compiler_params=pltpu.CompilerParams(vmem_limit_bytes=LIMIT),
        cost_estimate=pl.CostEstimate(flops=entries * 2000, bytes_accessed=4 * cols.size, transcendentals=2 * entries),
        name="block_last" if last else "block_first",
    )(*((rows, cols, total) if last else (rows, cols)))


def body(points, inv_length, probes, noise):
    n_cols = lax.axis_size(COL_AXES)
    (dims, width), n_probes = points.shape, probes.shape[0]
    per = dims + n_probes
    f32 = jnp.float32
    row, cols = pl.pallas_call(
        prepare_kernel,
        out_shape=(
            jax.ShapeDtypeStruct((UNIT, width), f32),
            jax.ShapeDtypeStruct((n_cols * per, width), f32),
        ),
        in_specs=[WHOLE] * 3,
        out_specs=(WHOLE, WHOLE),
        compiler_params=pltpu.CompilerParams(vmem_limit_bytes=PREPARE_LIMIT),
        name="prepare",
    )(points, inv_length[None, :], probes)
    cols = lax.all_to_all(cols.reshape(n_cols * per, 1, width), COL_AXES, 0, 0, tiled=True).reshape(n_cols * per, width)
    other = lax.ppermute(cols, "c", [(0, 1), (1, 0)])
    rows = lax.all_gather(row, ROW_AXES, axis=0)
    total, turned = block(rows, cols, dims, n_probes)
    part = block(turned, other, dims, n_probes, total)
    part = lax.all_to_all(part, ROW_AXES, 0, 0, tiled=True)
    return jnp.sum(part, axis=0) + noise[0] * probes


def solution(mesh):
    fine = Mesh(mesh.devices.reshape(4, 4, 2, 4, 4), AXES)
    split = P(None, AXES)
    return jax.shard_map(body, mesh=fine, in_specs=(split, P(), split, P()), out_specs=split, check_vma=False)
```

```python
import functools
import math

import jax
import jax.numpy as jnp
from jax import lax
from jax.experimental import pallas as pl
from jax.experimental.pallas import tpu as pltpu
from jax.sharding import Mesh, PartitionSpec as P

AXES = ("x", "zl", "c", "y", "zh")
COL_AXES = ("zl", "zh")
ROW_AXES = ("x", "y")
LANES = 128
UNIT = 16
DEPTH = 128
TILE = 256
STEP = 32
SCALE = math.sqrt(5.0) / 3.0
RATE = -3.0 / math.log(2.0)
TINY = 1e-30
PREPARE_LIMIT = 60 * 1024 * 1024
LIMIT = 32 * 1024 * 1024
WHOLE = pl.BlockSpec(memory_space=pltpu.VMEM)


def extended(x, norm, one, ref):
    dims = x.shape[0]
    ref[...] = jnp.zeros(ref.shape, jnp.float32)
    ref[0:dims] = x
    ref[dims : dims + 1] = norm
    ref[dims + 1 : dims + 2] = one


def prepare_kernel(points_ref, length_ref, probes_ref, row_ref, cols_ref):
    dims, n_probes = points_ref.shape[0], probes_ref.shape[0]
    at = lax.broadcasted_iota(jnp.int32, (dims, dims), 0) == lax.broadcasted_iota(jnp.int32, (dims, dims), 1)
    length = jnp.sum(jnp.where(at, length_ref[...], 0.0), axis=1, keepdims=True)
    x = points_ref[...] * (length * SCALE)
    norm = jnp.sum(x * x, axis=0, keepdims=True)
    extended(x, norm, jnp.ones_like(norm), row_ref)
    probes = probes_ref[...]
    for start in range(0, cols_ref.shape[0], dims + n_probes):
        cols_ref[start : start + dims] = x
        cols_ref[start + dims : start + dims + n_probes] = probes


def split3(value):
    first = value.astype(jnp.bfloat16)
    rest = value - first.astype(jnp.float32)
    second = rest.astype(jnp.bfloat16)
    third = (rest - second.astype(jnp.float32)).astype(jnp.bfloat16)
    return first, second, third


def halves(squared):
    squared = jnp.maximum(squared, TINY)
    v = squared * lax.rsqrt(squared)
    k = ((squared + v) + (1.0 / 3.0)) * jnp.exp2(v * RATE)
    high = k.astype(jnp.bfloat16)
    return high, (k - high.astype(jnp.float32)).astype(jnp.bfloat16)


def block_kernel(last, dims, *refs):
    if last:
        a, cols_ref, sum_ref, out_ref, b, q, unit, d0, d1, h0, h1, acc = refs
        n_probes = out_ref.shape[1]
    else:
        rows_ref, cols_ref, acc, a, b, q, unit, d0, d1, h0, h1 = refs
        n_probes = acc.shape[1] // 2
    d, h = (d0, d1), (h0, h1)
    per = dims + n_probes
    n_rows, n_cols = a.shape[0] * TILE // LANES, cols_ref.shape[0] // per
    each = TILE // LANES
    span = b.shape[1]
    wide = span // LANES
    zero = jnp.zeros((UNIT, LANES), jnp.bfloat16)

    if not last:
        for s in range(n_rows):
            u1, u2, u3 = split3(rows_ref[s])
            lanes = slice((s % each) * LANES, (s % each + 1) * LANES)
            a[s // each, :, lanes] = jnp.concatenate([u1, u1, u2, u2, u1, u3, zero, zero], axis=0)
    for s in range(n_cols):
        x = cols_ref[s * per : s * per + dims]
        norm = jnp.sum(x * x, axis=0, keepdims=True)
        extended(-2.0 * x, jnp.ones_like(norm), norm, unit.at[s])
        v1, v2, v3 = split3(unit[s])
        lanes = slice((s % wide) * LANES, (s % wide + 1) * LANES)
        stack = jnp.concatenate([v1, v2, v1, v2, v3, v1, zero, zero], axis=0)
        b[s // wide, lanes, :] = stack.T
        p = cols_ref[s * per + dims : (s + 1) * per]
        p1 = p.astype(jnp.bfloat16)
        p2 = (p - p1.astype(jnp.float32)).astype(jnp.bfloat16)
        both = jnp.concatenate([p1, p2], axis=0)
        q[s // wide, :, lanes] = both
        q[s // wide, :, lanes.start + span : lanes.stop + span] = both
    tiles, chunks = a.shape[0], b.shape[0]
    count = tiles * chunks

    def distance(at):
        return jnp.dot(b[at // tiles], a[at % tiles], preferred_element_type=jnp.float32)

    def product(at):
        return jnp.dot(q[at // tiles], h[at % 2][...], preferred_element_type=jnp.float32)

    def add(at, value):
        tile = at % tiles
        if at >= tiles:
            value = acc[tile] + value
        elif last:
            value = sum_ref[tile] + value
        if not last or at < count - tiles:
            acc[tile] = value
            return
        value = 3.0 * (value[0:n_probes] + value[n_probes:])
        for s in range(each):
            out_ref[tile * each + s] = value[:, s * LANES : (s + 1) * LANES]

    def covariance(at, start, stop):
        for r in range(start, stop, STEP):
            high, low = halves(d[at % 2][r : r + STEP])
            h[at % 2][r : r + STEP] = high
            h[at % 2][span + r : span + r + STEP] = low

    d0[...] = distance(0)
    for at in range(count):
        early = 0 if last or at == 0 else span // 2
        if at > 0:
            before = product(at - 1)
            covariance(at, 0, early)
            add(at - 1, before)
        if at + 1 < count:
            d[1 - at % 2][...] = distance(at + 1)
        covariance(at, early, span)
    add(count - 1, product(count - 1))


def block(rows, cols, dims, n_probes, total=None):
    f32, bf16 = jnp.float32, jnp.bfloat16
    last = total is not None
    n_rows = rows.shape[0] * TILE // LANES if last else rows.shape[0]
    n_cols = cols.shape[0] // (dims + n_probes)
    span = 2 * TILE
    row_tiles, col_tiles = n_rows * LANES // TILE, n_cols * LANES // span
    sums = jax.ShapeDtypeStruct((row_tiles, 2 * n_probes, TILE), f32)
    turned = jax.ShapeDtypeStruct((row_tiles, DEPTH, TILE), bf16)
    entries = n_rows * n_cols * LANES * LANES
    return pl.pallas_call(
        functools.partial(block_kernel, last, dims),
        out_shape=jax.ShapeDtypeStruct((n_rows, n_probes, LANES), f32) if last else (sums, turned),
        in_specs=[WHOLE] * (3 if last else 2),
        out_specs=WHOLE if last else (WHOLE, WHOLE),
        scratch_shapes=[
            pltpu.VMEM((col_tiles, span, DEPTH), bf16),
            pltpu.VMEM((col_tiles, 2 * n_probes, 2 * span), bf16),
            pltpu.VMEM((n_cols, UNIT, LANES), f32),
            pltpu.VMEM((span, TILE), f32),
            pltpu.VMEM((span, TILE), f32),
            pltpu.VMEM((2 * span, TILE), bf16),
            pltpu.VMEM((2 * span, TILE), bf16),
        ]
        + [pltpu.VMEM(sums.shape, f32)] * last,
        compiler_params=pltpu.CompilerParams(vmem_limit_bytes=LIMIT),
        cost_estimate=pl.CostEstimate(flops=entries * 2000, bytes_accessed=4 * cols.size, transcendentals=2 * entries),
        name="block_last" if last else "block_first",
    )(*((rows, cols, total) if last else (rows, cols)))


def body(points, inv_length, probes, noise):
    n_cols = lax.axis_size(COL_AXES)
    (dims, width), n_probes = points.shape, probes.shape[0]
    per = dims + n_probes
    f32 = jnp.float32
    row, cols = pl.pallas_call(
        prepare_kernel,
        out_shape=(
            jax.ShapeDtypeStruct((UNIT, width), f32),
            jax.ShapeDtypeStruct((n_cols * per, width), f32),
        ),
        in_specs=[WHOLE] * 3,
        out_specs=(WHOLE, WHOLE),
        compiler_params=pltpu.CompilerParams(vmem_limit_bytes=PREPARE_LIMIT),
        name="prepare",
    )(points, inv_length[None, :], probes)
    cols = lax.all_to_all(cols.reshape(n_cols * per, 1, width), COL_AXES, 0, 0, tiled=True).reshape(n_cols * per, width)
    other = lax.ppermute(cols, "c", [(0, 1), (1, 0)])
    rows = lax.all_gather(row, ROW_AXES, axis=0)
    total, turned = block(rows, cols, dims, n_probes)
    part = block(turned, other, dims, n_probes, total)
    part = lax.all_to_all(part, ROW_AXES, 0, 0, tiled=True)
    return jnp.sum(part, axis=0) + noise[0] * probes


def solution(mesh):
    fine = Mesh(mesh.devices.reshape(4, 4, 2, 4, 4), AXES)
    split = P(None, AXES)
    return jax.shard_map(body, mesh=fine, in_specs=(split, P(), split, P()), out_specs=split, check_vma=False)
```

```python
import functools
import math

import jax
import jax.numpy as jnp
from jax import lax
from jax.experimental import pallas as pl
from jax.experimental.pallas import tpu as pltpu
from jax.sharding import Mesh, PartitionSpec as P

AXES = ("x", "zl", "c", "y", "zh")
COL_AXES = ("zl", "zh")
ROW_AXES = ("x", "y")
LANES = 128
UNIT = 16
DEPTH = 128
TILE = 256
STEP = 32
SCALE = math.sqrt(5.0) / 3.0
RATE = -3.0 / math.log(2.0)
TINY = 1e-30
PREPARE_LIMIT = 60 * 1024 * 1024
LIMIT = 32 * 1024 * 1024
WHOLE = pl.BlockSpec(memory_space=pltpu.VMEM)


def extended(x, norm, one, ref):
    dims = x.shape[0]
    ref[...] = jnp.zeros(ref.shape, jnp.float32)
    ref[0:dims] = x
    ref[dims : dims + 1] = norm
    ref[dims + 1 : dims + 2] = one


def prepare_kernel(points_ref, length_ref, probes_ref, row_ref, cols_ref):
    dims, n_probes = points_ref.shape[0], probes_ref.shape[0]
    at = lax.broadcasted_iota(jnp.int32, (dims, dims), 0) == lax.broadcasted_iota(jnp.int32, (dims, dims), 1)
    length = jnp.sum(jnp.where(at, length_ref[...], 0.0), axis=1, keepdims=True)
    x = points_ref[...] * (length * SCALE)
    norm = jnp.sum(x * x, axis=0, keepdims=True)
    extended(x, norm, jnp.ones_like(norm), row_ref)
    probes = probes_ref[...]
    for start in range(0, cols_ref.shape[0], dims + n_probes):
        cols_ref[start : start + dims] = x
        cols_ref[start + dims : start + dims + n_probes] = probes


def split3(value):
    first = value.astype(jnp.bfloat16)
    rest = value - first.astype(jnp.float32)
    second = rest.astype(jnp.bfloat16)
    third = (rest - second.astype(jnp.float32)).astype(jnp.bfloat16)
    return first, second, third


def halves(squared):
    squared = jnp.maximum(squared, TINY)
    v = squared * lax.rsqrt(squared)
    k = ((squared + v) + (1.0 / 3.0)) * jnp.exp2(v * RATE)
    high = k.astype(jnp.bfloat16)
    return high, (k - high.astype(jnp.float32)).astype(jnp.bfloat16)


def block_kernel(last, dims, *refs):
    if last:
        a, cols_ref, sum_ref, out_ref, b, q, unit, d0, d1, h0, h1, acc = refs
        n_probes = out_ref.shape[1]
    else:
        rows_ref, cols_ref, acc, a, b, q, unit, d0, d1, h0, h1 = refs
        n_probes = acc.shape[1] // 2
    d, h = (d0, d1), (h0, h1)
    per = dims + n_probes
    n_rows, n_cols = a.shape[0] * TILE // LANES, cols_ref.shape[0] // per
    each = TILE // LANES
    span = b.shape[1]
    wide = span // LANES
    zero = jnp.zeros((UNIT, LANES), jnp.bfloat16)

    if not last:
        for s in range(n_rows):
            u1, u2, u3 = split3(rows_ref[s])
            lanes = slice((s % each) * LANES, (s % each + 1) * LANES)
            a[s // each, :, lanes] = jnp.concatenate([u1, u1, u2, u2, u1, u3, zero, zero], axis=0)
    for s in range(n_cols):
        x = cols_ref[s * per : s * per + dims]
        norm = jnp.sum(x * x, axis=0, keepdims=True)
        extended(-2.0 * x, jnp.ones_like(norm), norm, unit.at[s])
        v1, v2, v3 = split3(unit[s])
        lanes = slice((s % wide) * LANES, (s % wide + 1) * LANES)
        stack = jnp.concatenate([v1, v2, v1, v2, v3, v1, zero, zero], axis=0)
        b[s // wide, lanes, :] = stack.T
        p = cols_ref[s * per + dims : (s + 1) * per]
        p1 = p.astype(jnp.bfloat16)
        p2 = (p - p1.astype(jnp.float32)).astype(jnp.bfloat16)
        both = jnp.concatenate([p1, p2], axis=0)
        q[s // wide, :, lanes] = both
        q[s // wide, :, lanes.start + span : lanes.stop + span] = both
    tiles, chunks = a.shape[0], b.shape[0]
    count = tiles * chunks

    def distance(at):
        return jnp.dot(b[at // tiles], a[at % tiles], preferred_element_type=jnp.float32)

    def product(at):
        return jnp.dot(q[at // tiles], h[at % 2][...], preferred_element_type=jnp.float32)

    def add(at, value):
        tile = at % tiles
        if at >= tiles:
            value = acc[tile] + value
        elif last:
            value = sum_ref[tile] + value
        if not last or at < count - tiles:
            acc[tile] = value
            return
        value = 3.0 * (value[0:n_probes] + value[n_probes:])
        for s in range(each):
            out_ref[tile * each + s] = value[:, s * LANES : (s + 1) * LANES]

    def covariance(at, start, stop):
        for r in range(start, stop, STEP):
            high, low = halves(d[at % 2][r : r + STEP])
            h[at % 2][r : r + STEP] = high
            h[at % 2][span + r : span + r + STEP] = low

    d0[...] = distance(0)
    for at in range(count):
        early = 0 if last or at == 0 else span // 2
        if at > 0:
            before = product(at - 1)
            covariance(at, 0, early)
            add(at - 1, before)
        if at + 1 < count:
            d[1 - at % 2][...] = distance(at + 1)
        covariance(at, early, span)
    add(count - 1, product(count - 1))


def block(rows, cols, dims, n_probes, total=None):
    f32, bf16 = jnp.float32, jnp.bfloat16
    last = total is not None
    n_rows = rows.shape[0] * TILE // LANES if last else rows.shape[0]
    n_cols = cols.shape[0] // (dims + n_probes)
    span = 4 * TILE
    row_tiles, col_tiles = n_rows * LANES // TILE, n_cols * LANES // span
    sums = jax.ShapeDtypeStruct((row_tiles, 2 * n_probes, TILE), f32)
    turned = jax.ShapeDtypeStruct((row_tiles, DEPTH, TILE), bf16)
    entries = n_rows * n_cols * LANES * LANES
    return pl.pallas_call(
        functools.partial(block_kernel, last, dims),
        out_shape=jax.ShapeDtypeStruct((n_rows, n_probes, LANES), f32) if last else (sums, turned),
        in_specs=[WHOLE] * (3 if last else 2),
        out_specs=WHOLE if last else (WHOLE, WHOLE),
        scratch_shapes=[
            pltpu.VMEM((col_tiles, span, DEPTH), bf16),
            pltpu.VMEM((col_tiles, 2 * n_probes, 2 * span), bf16),
            pltpu.VMEM((n_cols, UNIT, LANES), f32),
            pltpu.VMEM((span, TILE), f32),
            pltpu.VMEM((span, TILE), f32),
            pltpu.VMEM((2 * span, TILE), bf16),
            pltpu.VMEM((2 * span, TILE), bf16),
        ]
        + [pltpu.VMEM(sums.shape, f32)] * last,
        compiler_params=pltpu.CompilerParams(vmem_limit_bytes=LIMIT),
        cost_estimate=pl.CostEstimate(flops=entries * 2000, bytes_accessed=4 * cols.size, transcendentals=2 * entries),
        name="block_last" if last else "block_first",
    )(*((rows, cols, total) if last else (rows, cols)))


def body(points, inv_length, probes, noise):
    n_cols = lax.axis_size(COL_AXES)
    (dims, width), n_probes = points.shape, probes.shape[0]
    per = dims + n_probes
    f32 = jnp.float32
    row, cols = pl.pallas_call(
        prepare_kernel,
        out_shape=(
            jax.ShapeDtypeStruct((UNIT, width), f32),
            jax.ShapeDtypeStruct((n_cols * per, width), f32),
        ),
        in_specs=[WHOLE] * 3,
        out_specs=(WHOLE, WHOLE),
        compiler_params=pltpu.CompilerParams(vmem_limit_bytes=PREPARE_LIMIT),
        name="prepare",
    )(points, inv_length[None, :], probes)
    cols = lax.all_to_all(cols.reshape(n_cols * per, 1, width), COL_AXES, 0, 0, tiled=True).reshape(n_cols * per, width)
    other = lax.ppermute(cols, "c", [(0, 1), (1, 0)])
    rows = lax.all_gather(row, ROW_AXES, axis=0)
    total, turned = block(rows, cols, dims, n_probes)
    part = block(turned, other, dims, n_probes, total)
    part = lax.all_to_all(part, ROW_AXES, 0, 0, tiled=True)
    return jnp.sum(part, axis=0) + noise[0] * probes


def solution(mesh):
    fine = Mesh(mesh.devices.reshape(4, 4, 2, 4, 4), AXES)
    split = P(None, AXES)
    return jax.shard_map(body, mesh=fine, in_specs=(split, P(), split, P()), out_specs=split, check_vma=False)
```

```python
import functools
import math

import jax
import jax.numpy as jnp
from jax import lax
from jax.experimental import pallas as pl
from jax.experimental.pallas import tpu as pltpu
from jax.sharding import Mesh, PartitionSpec as P

AXES = ("x", "zl", "c", "y", "zh")
COL_AXES = ("zl", "zh")
ROW_AXES = ("x", "y")
LANES = 128
UNIT = 16
DEPTH = 128
TILE = 256
STEP = 32
SCALE = math.sqrt(5.0) / 3.0
RATE = -3.0 / math.log(2.0)
TINY = 1e-30
PREPARE_LIMIT = 60 * 1024 * 1024
LIMIT = 32 * 1024 * 1024
WHOLE = pl.BlockSpec(memory_space=pltpu.VMEM)


def extended(x, norm, one, ref):
    dims = x.shape[0]
    ref[...] = jnp.zeros(ref.shape, jnp.float32)
    ref[0:dims] = x
    ref[dims : dims + 1] = norm
    ref[dims + 1 : dims + 2] = one


def prepare_kernel(points_ref, length_ref, probes_ref, row_ref, cols_ref):
    dims, n_probes = points_ref.shape[0], probes_ref.shape[0]
    at = lax.broadcasted_iota(jnp.int32, (dims, dims), 0) == lax.broadcasted_iota(jnp.int32, (dims, dims), 1)
    length = jnp.sum(jnp.where(at, length_ref[...], 0.0), axis=1, keepdims=True)
    x = points_ref[...] * (length * SCALE)
    norm = jnp.sum(x * x, axis=0, keepdims=True)
    extended(x, norm, jnp.ones_like(norm), row_ref)
    probes = probes_ref[...]
    for start in range(0, cols_ref.shape[0], dims + n_probes):
        cols_ref[start : start + dims] = x
        cols_ref[start + dims : start + dims + n_probes] = probes


def split3(value):
    first = value.astype(jnp.bfloat16)
    rest = value - first.astype(jnp.float32)
    second = rest.astype(jnp.bfloat16)
    third = (rest - second.astype(jnp.float32)).astype(jnp.bfloat16)
    return first, second, third


def halves(squared):
    squared = jnp.maximum(squared, TINY)
    v = squared * lax.rsqrt(squared)
    k = ((squared + v) + (1.0 / 3.0)) * jnp.exp2(v * RATE)
    high = k.astype(jnp.bfloat16)
    return high, (k - high.astype(jnp.float32)).astype(jnp.bfloat16)


def block_kernel(last, dims, *refs):
    if last:
        a, cols_ref, sum_ref, out_ref, b, q, unit, d0, d1, h0, h1, acc = refs
        n_probes = out_ref.shape[1]
    else:
        rows_ref, cols_ref, acc, a, b, q, unit, d0, d1, h0, h1 = refs
        n_probes = acc.shape[1] // 2
    d, h = (d0, d1), (h0, h1)
    per = dims + n_probes
    n_rows, n_cols = a.shape[0] * TILE // LANES, cols_ref.shape[0] // per
    each = TILE // LANES
    span = b.shape[1]
    wide = span // LANES
    zero = jnp.zeros((UNIT, LANES), jnp.bfloat16)

    if not last:
        for s in range(n_rows):
            u1, u2, u3 = split3(rows_ref[s])
            lanes = slice((s % each) * LANES, (s % each + 1) * LANES)
            a[s // each, :, lanes] = jnp.concatenate([u1, u1, u2, u2, u1, u3, zero, zero], axis=0)
    for s in range(n_cols):
        x = cols_ref[s * per : s * per + dims]
        norm = jnp.sum(x * x, axis=0, keepdims=True)
        extended(-2.0 * x, jnp.ones_like(norm), norm, unit.at[s])
        v1, v2, v3 = split3(unit[s])
        lanes = slice((s % wide) * LANES, (s % wide + 1) * LANES)
        stack = jnp.concatenate([v1, v2, v1, v2, v3, v1, zero, zero], axis=0)
        b[s // wide, lanes, :] = stack.T
        p = cols_ref[s * per + dims : (s + 1) * per]
        p1 = p.astype(jnp.bfloat16)
        p2 = (p - p1.astype(jnp.float32)).astype(jnp.bfloat16)
        both = jnp.concatenate([p1, p2], axis=0)
        q[s // wide, :, lanes] = both
        q[s // wide, :, lanes.start + span : lanes.stop + span] = both
    tiles, chunks = a.shape[0], b.shape[0]
    count = tiles * chunks

    def distance(at):
        return jnp.dot(b[at // tiles], a[at % tiles], preferred_element_type=jnp.float32)

    def product(at):
        return jnp.dot(q[at // tiles], h[at % 2][...], preferred_element_type=jnp.float32)

    def add(at, value):
        tile = at % tiles
        if at >= tiles:
            value = acc[tile] + value
        elif last:
            value = sum_ref[tile] + value
        if not last or at < count - tiles:
            acc[tile] = value
            return
        value = 3.0 * (value[0:n_probes] + value[n_probes:])
        for s in range(each):
            out_ref[tile * each + s] = value[:, s * LANES : (s + 1) * LANES]

    def covariance(at, start, stop):
        for r in range(start, stop, STEP):
            high, low = halves(d[at % 2][r : r + STEP])
            h[at % 2][r : r + STEP] = high
            h[at % 2][span + r : span + r + STEP] = low

    d0[...] = distance(0)
    for at in range(count):
        early = 0 if last or at == 0 else span // 2
        if at > 0:
            before = product(at - 1)
            covariance(at, 0, early)
            add(at - 1, before)
        if at + 1 < count:
            d[1 - at % 2][...] = distance(at + 1)
        covariance(at, early, span)
    add(count - 1, product(count - 1))


def block(rows, cols, dims, n_probes, total=None):
    f32, bf16 = jnp.float32, jnp.bfloat16
    last = total is not None
    n_rows = rows.shape[0] * TILE // LANES if last else rows.shape[0]
    n_cols = cols.shape[0] // (dims + n_probes)
    span = 4 * TILE if last else 2 * TILE
    row_tiles, col_tiles = n_rows * LANES // TILE, n_cols * LANES // span
    sums = jax.ShapeDtypeStruct((row_tiles, 2 * n_probes, TILE), f32)
    turned = jax.ShapeDtypeStruct((row_tiles, DEPTH, TILE), bf16)
    entries = n_rows * n_cols * LANES * LANES
    return pl.pallas_call(
        functools.partial(block_kernel, last, dims),
        out_shape=jax.ShapeDtypeStruct((n_rows, n_probes, LANES), f32) if last else (sums, turned),
        in_specs=[WHOLE] * (3 if last else 2),
        out_specs=WHOLE if last else (WHOLE, WHOLE),
        scratch_shapes=[
            pltpu.VMEM((col_tiles, span, DEPTH), bf16),
            pltpu.VMEM((col_tiles, 2 * n_probes, 2 * span), bf16),
            pltpu.VMEM((n_cols, UNIT, LANES), f32),
            pltpu.VMEM((span, TILE), f32),
            pltpu.VMEM((span, TILE), f32),
            pltpu.VMEM((2 * span, TILE), bf16),
            pltpu.VMEM((2 * span, TILE), bf16),
        ]
        + [pltpu.VMEM(sums.shape, f32)] * last,
        compiler_params=pltpu.CompilerParams(vmem_limit_bytes=LIMIT),
        cost_estimate=pl.CostEstimate(flops=entries * 2000, bytes_accessed=4 * cols.size, transcendentals=2 * entries),
        name="block_last" if last else "block_first",
    )(*((rows, cols, total) if last else (rows, cols)))


def body(points, inv_length, probes, noise):
    n_cols = lax.axis_size(COL_AXES)
    (dims, width), n_probes = points.shape, probes.shape[0]
    per = dims + n_probes
    f32 = jnp.float32
    row, cols = pl.pallas_call(
        prepare_kernel,
        out_shape=(
            jax.ShapeDtypeStruct((UNIT, width), f32),
            jax.ShapeDtypeStruct((n_cols * per, width), f32),
        ),
        in_specs=[WHOLE] * 3,
        out_specs=(WHOLE, WHOLE),
        compiler_params=pltpu.CompilerParams(vmem_limit_bytes=PREPARE_LIMIT),
        name="prepare",
    )(points, inv_length[None, :], probes)
    cols = lax.all_to_all(cols.reshape(n_cols * per, 1, width), COL_AXES, 0, 0, tiled=True).reshape(n_cols * per, width)
    other = lax.ppermute(cols, "c", [(0, 1), (1, 0)])
    rows = lax.all_gather(row, ROW_AXES, axis=0)
    total, turned = block(rows, cols, dims, n_probes)
    part = block(turned, other, dims, n_probes, total)
    part = lax.all_to_all(part, ROW_AXES, 0, 0, tiled=True)
    return jnp.sum(part, axis=0) + noise[0] * probes


def solution(mesh):
    fine = Mesh(mesh.devices.reshape(4, 4, 2, 4, 4), AXES)
    split = P(None, AXES)
    return jax.shard_map(body, mesh=fine, in_specs=(split, P(), split, P()), out_specs=split, check_vma=False)
```
